32 devices in a mesh: rep: 1, ep: 32 (over z, y, x, core), hid: 1.
Axes of the slice: x: 2, y: 2, z: 4, core: 2. Of those that a mesh axis runs over, the one named last changes fastest.
Arguments:
- tokens: bfloat16 [4096, 2048], P(('rep', 'ep')), may hold values from -6 to 6
- cotangent: bfloat16 [4096, 2048], P(('rep', 'ep')), may hold values from -2 to 2
- routing: float32 [4096, 8], P(('rep', 'ep')), may hold values from 0.05 to 0.5
- expert_ids: int32 [4096, 8], P(('rep', 'ep')), may hold values from 0 to 63, all different within a row; in each aligned block of 128 rows (0 to 127, 128 to 255, ...) at most 20 rows name the same one
- gate_weight: bfloat16 [64, 2048, 768], P('ep', None, 'hid'), may hold values from -0.125 to 0.125
- up_weight: bfloat16 [64, 2048, 768], P('ep', None, 'hid'), may hold values from -0.125 to 0.125
- down_weight: bfloat16 [64, 768, 2048], P('ep', 'hid'), may hold values from -0.21875 to 0.21875
Outputs:
- input_grad: float32 [4096, 2048], P(('rep', 'ep'), 'hid')
- gate_grad: float32 [4096, 8], P(('rep', 'ep'))
The draws below stay inside these ranges and needn't reach their ends.
Inputs may be any that keep to these rules, and one draw needn't show every extreme that they name: `expert_ids`: among the 128 tokens of one index of ep (aligned blocks of rows), no expert is picked more than 20 times, a bound that some block reaches; the 8 picks of a token are different experts.
All inputs are finite; a program needn't handle non-finite values.
Results may differ from the reference program's by a relative error of at most 0.0029.
Values may be sent and summed in bfloat16 or wider, within the bound.
No kernel may reach another device: no remote copies, remote signals or barrier semaphores. Data moves between devices by JAX's collectives and lax.ppermute only.
A program may use at most 128 MiB of HBM per device.

```python
import math
import jax
import jax.numpy as jnp
import numpy as np
from jax import lax

D = 2048
FF = 768
TOP = 8
TOK_DEV = 128
EXPERTS = 64
TOKENS = 4096
CAP = 20
N_EP = 32


def levels(rng, shape, split, smallest, high):
    factor_of, own = 1.0, jax.random.fold_in(rng, 6)
    for position, parts in split:
        heights = jnp.exp(jax.random.uniform(jax.random.fold_in(own, position), (parts,), jnp.float32, smallest / len(split), high / len(split)))
        factor_of = factor_of * jnp.repeat(heights, shape[position] // parts).reshape([-1 if axis == position else 1 for axis in range(len(shape))])
    return factor_of


def deal_out(own_key, own, number, rows, count, top, bound, skew):
    ranking = jax.random.permutation(own_key, count)
    crowded, common = load_shares(count, rows * top, bound, skew, True), load_shares(count, rows * top, bound, skew, False)
    places = jnp.arange(count)

    def named(sizes, offset_by):
        used = int((sizes > 0).sum())
        fixed = max(1, used // 4)
        moved = fixed + (places - fixed + offset_by * (used - fixed)) % max(1, count - fixed)
        return jnp.zeros((count,), jnp.int32).at[ranking[jnp.where(places < fixed, places, moved)]].set(jnp.asarray(sizes, jnp.int32))

    sizes = jnp.where(number % 4 == 0, named(crowded, number // 4), named(common, number - number // 4 - 1))
    mixed = jax.random.permutation(jax.random.fold_in(own, 3), count)
    source_of, receiver = mixed[0:count // 2 * 2:2], mixed[1:count // 2 * 2:2]
    slack = jnp.minimum(sizes[source_of] - 1, bound - sizes[receiver]) // 2
    slack = jnp.where((source_of == ranking[0]) | (receiver == ranking[0]) | (sizes[receiver] == 0), 0, jnp.maximum(slack, 0))
    moved = jax.random.randint(jax.random.fold_in(own, 4), (count // 2,), 0, 1 << 20) % (slack + 1)
    sizes = sizes.at[source_of].add(-moved).at[receiver].add(moved)
    items = jnp.searchsorted(jnp.cumsum(sizes), jnp.arange(rows * top), side="right").astype(jnp.int32)
    table = items.reshape(top, rows).T
    table = table[jax.random.permutation(jax.random.fold_in(own, 1), rows)]
    offset_by = jax.random.randint(jax.random.fold_in(own, 2), (rows, 1), 0, top)
    return jnp.take_along_axis(table, (jnp.arange(top)[None, :] + offset_by) % top, axis=1)


def load_shares(number_of, total, most, lean, full):
    weights = [(1 << 20) // math.isqrt(rank ** lean) + 1 for rank in range(1, number_of + 1)]
    largest = most if full else min(most, max(-(-total // number_of), total * weights[0] // sum(weights)))
    least = 1 if total - largest >= number_of - 1 else 0
    holding, spare = [largest] + [least] * (number_of - 1), total - largest - least * (number_of - 1)
    while spare > 0:
        candidates = [i for i in range(1, number_of) if holding[i] < largest] or [i for i in range(1, number_of) if holding[i] < most]
        whole, left = sum([weights[i] for i in candidates]), spare
        for i in candidates:
            more = min(most - holding[i], max(1, left * weights[i] // whole), spare)
            holding[i] = holding[i] + more
            spare = spare - more
    return np.array(holding)


def bell_draw(rng, dims, deviation, bound, pieces=(), kind=jnp.bfloat16):
    gain = levels(rng, dims, pieces, -0.22, 0.18) if pieces else 1.0
    entries = jax.random.normal(rng, dims, jnp.float32) * deviation * gain
    return jnp.minimum(jnp.maximum(entries, -bound), bound).astype(kind)


def setup_inputs(seed: int = 0, part: int = 0) -> dict:
    arg_keys = jax.random.split(jax.random.key(seed), 8)
    own_keys = jax.random.split(jax.random.fold_in(arg_keys[7], part), 8)
    tokens = bell_draw(own_keys[0], (TOKENS, D), 1.0, 6.0, ((0, 32),))
    cotangent = bell_draw(own_keys[1], (TOKENS, D), 0.3, 2.0, ((0, 32),))
    routing = jnp.clip(jnp.exp(math.log(0.5) - 2.3025851 * jax.random.uniform(own_keys[2], (TOKENS, TOP), jnp.float32) ** levels(own_keys[2], (TOKENS, TOP), ((0, 32),), -0.2, 0.2)), 0.05, 0.5)
    expert_ids_keys = jax.random.split(jax.random.fold_in(own_keys[3], 1), TOKENS // TOK_DEV)
    expert_ids_turns = jax.random.permutation(jax.random.fold_in(own_keys[3], 3), TOKENS // TOK_DEV)
    expert_ids = jax.vmap(lambda own, number: deal_out(jax.random.fold_in(own_keys[3], 2), own, number, TOK_DEV, EXPERTS, TOP, CAP, 1))(expert_ids_keys, expert_ids_turns).reshape((TOKENS, TOP))
    gate_weight = bell_draw(arg_keys[4], (EXPERTS, D, FF), D ** -0.5, 0.125, ((0, 32),))
    up_weight = bell_draw(arg_keys[5], (EXPERTS, D, FF), D ** -0.5, 0.125, ((0, 32),))
    down_weight = bell_draw(arg_keys[6], (EXPERTS, FF, D), FF ** -0.5, 0.21875, ((0, 32),))
    return dict(tokens=tokens, cotangent=cotangent, routing=routing, expert_ids=expert_ids, gate_weight=gate_weight, up_weight=up_weight, down_weight=down_weight)


def slot_rank(flat, experts):
    onehot = (flat[:, None] == jnp.arange(experts, dtype=jnp.int32)[None, :]).astype(jnp.int32)
    before = jnp.cumsum(onehot, axis=0) - onehot
    return jnp.sum(before * onehot, axis=1).astype(jnp.int32)


def reference(tokens, cotangent, routing, expert_ids, gate_weight, up_weight, down_weight):
    picks = TOK_DEV * TOP
    rows_expert = N_EP * CAP
    id_blocks = expert_ids.reshape(N_EP, picks).astype(jnp.int32)
    ranks = jax.vmap(lambda flat: slot_rank(flat, EXPERTS))(id_blocks)
    source = jnp.arange(N_EP, dtype=jnp.int32)[:, None]
    slots = (id_blocks * rows_expert + source * CAP + ranks).reshape(-1).astype(jnp.int32)
    pick_index = jnp.arange(TOKENS * TOP, dtype=jnp.int32)
    token_index = (pick_index // TOP).astype(jnp.int32)
    slot_token = jnp.full((EXPERTS * rows_expert,), TOKENS, jnp.int32).at[slots].set(token_index)
    slot_pick = jnp.full((EXPERTS * rows_expert,), TOKENS * TOP, jnp.int32).at[slots].set(pick_index)
    padding = jnp.zeros((1, D), tokens.dtype)
    token_rows = jnp.concatenate([tokens, padding], 0)[slot_token].reshape(EXPERTS, rows_expert, D)
    cotan_rows = jnp.concatenate([cotangent, padding], 0)[slot_token].reshape(EXPERTS, rows_expert, D)
    weight_flat = jnp.concatenate([routing.reshape(-1), jnp.zeros((1,), jnp.float32)], 0)
    slot_weight = weight_flat[slot_pick].reshape(EXPERTS, rows_expert)
    slot_token = slot_token.reshape(EXPERTS, rows_expert)
    slot_pick = slot_pick.reshape(EXPERTS, rows_expert)

    def expert_step(carry, items):
        grad_sum, gate_sum = carry
        inputs, grads_in, w_gate, up_proj, w_down, target, pick_slot, weight = items
        gate_pre = jnp.dot(inputs, w_gate, preferred_element_type=jnp.float32)
        up_pre = jnp.dot(inputs, up_proj, preferred_element_type=jnp.float32)
        upward = jnp.dot(grads_in, w_down.T, preferred_element_type=jnp.float32)
        sigma = jax.nn.sigmoid(gate_pre)
        silu_val = gate_pre * sigma
        hidden = silu_val * up_pre
        pick_gate = jnp.sum(hidden * upward, axis=1)
        gate_delta = (upward * up_pre * sigma * (1.0 + gate_pre * (1.0 - sigma))).astype(jnp.bfloat16)
        up_delta = (upward * silu_val).astype(jnp.bfloat16)
        pick_grad = jnp.dot(gate_delta, w_gate.T, preferred_element_type=jnp.float32)
        pick_grad = pick_grad + jnp.dot(up_delta, up_proj.T, preferred_element_type=jnp.float32)
        grad_sum = grad_sum.at[target].add(weight[:, None] * pick_grad, mode="drop")
        gate_sum = gate_sum.at[pick_slot].add(pick_gate, mode="drop")
        return (grad_sum, gate_sum), None

    start = (jnp.zeros((TOKENS, D), jnp.float32), jnp.zeros((TOKENS * TOP,), jnp.float32))
    (grad_sum, gate_sum), _ = lax.scan(expert_step, start, (token_rows, cotan_rows, gate_weight, up_weight, down_weight, slot_token, slot_pick, slot_weight))
    return grad_sum, gate_sum.reshape(TOKENS, TOP)
```

```python
import functools
import math

import jax
import jax.numpy as jnp
from jax import lax
from jax.experimental import pallas as pl
from jax.experimental.pallas import tpu as pltpu
from jax.sharding import PartitionSpec as P

BF16 = jnp.bfloat16
F32 = jnp.float32
VMEM_LIMIT = 56 * 1024 * 1024


def full(shape):
    return pl.BlockSpec(shape, lambda *_: (0,) * len(shape))


def call(kernel, out_shape, grid, in_specs, out_specs, flops, moved, scratch=()):
    return pl.pallas_call(
        kernel,
        out_shape=out_shape,
        grid=grid,
        in_specs=in_specs,
        out_specs=out_specs,
        scratch_shapes=scratch,
        cost_estimate=pl.CostEstimate(flops=flops, bytes_accessed=moved, transcendentals=0),
        compiler_params=pltpu.CompilerParams(vmem_limit_bytes=VMEM_LIMIT),
    )


def picks_of(ids, base, experts):
    tokens, top = ids.shape
    expert = lax.broadcasted_iota(jnp.int32, (tokens, experts), 1).astype(F32) + base
    hits = [ids[:, k : k + 1] == expert for k in range(top)]
    return hits, functools.reduce(jnp.logical_or, hits)


def earlier_picks(pick):
    tokens = pick.shape[0]
    row = lax.broadcasted_iota(jnp.int32, (tokens, tokens), 0)
    column = lax.broadcasted_iota(jnp.int32, (tokens, tokens), 1)
    below = jnp.where(column < row, 1.0, 0.0).astype(BF16)
    return jnp.dot(below, jnp.where(pick, 1.0, 0.0).astype(BF16), preferred_element_type=F32)


def plan_kernel(owned, parts, capacity, base_ref, meta_ref, pack_ref, high_ref, low_ref):
    tokens = meta_ref.shape[1]
    slots = pack_ref.shape[0]
    experts = slots // (parts * capacity)
    top = meta_ref.shape[2] // 2
    base = base_ref[0, 0]
    slot = lax.broadcasted_iota(jnp.int32, (1, slots), 1)
    rank_of = (slot % capacity).astype(F32)
    part_of = (slot // capacity) % parts
    expert_of = slot // (capacity * parts)
    expert = lax.broadcasted_iota(jnp.int32, (experts, slots), 0)
    spread = jnp.where(expert == expert_of, 1.0, 0.0).astype(BF16)
    for part in range(parts):
        ids, routing = meta_ref[part, :, :top], meta_ref[part, :, top:]
        hits, pick = picks_of(ids, base, experts)
        weight = functools.reduce(
            jnp.add, [jnp.where(hits[k], routing[:, k : k + 1], 0.0) for k in range(top)]
        )
        rank = jnp.where(pick, earlier_picks(pick), -1.0).astype(BF16)
        high = weight.astype(BF16)
        low = (weight - high.astype(F32)).astype(BF16)
        ranks = jnp.dot(rank, spread, preferred_element_type=F32)
        here = jnp.logical_and(ranks == rank_of, part_of == part)
        rows = slice(part * tokens, (part + 1) * tokens)
        for out, value in ((high_ref, high), (low_ref, low)):
            spread_value = jnp.dot(value, spread, preferred_element_type=F32)
            out[rows, :] = jnp.where(here, spread_value, 0.0).astype(BF16)
        pack_ref[:, rows] = jnp.where(here, 1.0, 0.0).T.astype(BF16)


def plan(base, meta, owned, peers, capacity):
    parts, tokens, _ = meta.shape
    slots = peers * owned * parts * capacity
    rows = parts * tokens
    outs = (
        jax.ShapeDtypeStruct((slots, rows), BF16),
        jax.ShapeDtypeStruct((rows, slots), BF16),
        jax.ShapeDtypeStruct((rows, slots), BF16),
    )
    return call(
        functools.partial(plan_kernel, owned, parts, capacity),
        outs,
        (),
        [pl.BlockSpec(memory_space=pltpu.SMEM), pl.BlockSpec(memory_space=pltpu.VMEM)],
        [pl.BlockSpec(memory_space=pltpu.VMEM)] * 3,
        8 * slots * rows,
        6 * slots * rows,
    )(base, meta)


def pack_kernel(pack_ref, *refs):
    rows_refs, out_ref = refs[:-1], refs[-1]
    tokens = rows_refs[0].shape[0]
    total = None
    for part, ref in enumerate(rows_refs):
        term = jnp.dot(
            pack_ref[:, part * tokens : (part + 1) * tokens], ref[...], preferred_element_type=F32
        )
        total = term if total is None else total + term
    out_ref[...] = total.astype(out_ref.dtype)


def pack(matrix, rows):
    slots, sources = matrix.shape
    tokens, width = rows[0].shape
    block = math.gcd(width, 512)
    return call(
        pack_kernel,
        jax.ShapeDtypeStruct((slots, width), rows[0].dtype),
        (width // block,),
        [full((slots, sources))] + [pl.BlockSpec((tokens, block), lambda j: (0, j))] * len(rows),
        pl.BlockSpec((slots, block), lambda j: (0, j)),
        2 * slots * sources * width,
        2 * (slots + sources) * width,
    )(matrix, *rows)


def expert_kernel(pieces, token_ref, cotan_ref, gate_ref, up_ref, down_ref, *outs):
    peers, rows, width = token_ref.shape

    def joined(ref):
        return jnp.concatenate([ref[p].astype(F32) for p in range(peers)], axis=0).astype(BF16)

    inputs, grads_in = joined(token_ref), joined(cotan_ref)
    gate_pre = jnp.dot(inputs, gate_ref[...], preferred_element_type=F32)
    up_pre = jnp.dot(inputs, up_ref[...], preferred_element_type=F32)
    across = (((1,), (1,)), ((), ()))
    upward = lax.dot_general(grads_in, down_ref[...], across, preferred_element_type=F32)
    sigma = 1.0 / (1.0 + jnp.exp(-gate_pre))
    silu_val = gate_pre * sigma
    outs[-1][...] = jnp.sum(silu_val * up_pre * upward, axis=1, keepdims=True)
    gate_delta = (upward * up_pre * sigma * (1.0 + gate_pre * (1.0 - sigma))).astype(BF16)
    up_delta = (upward * silu_val).astype(BF16)
    step = width // pieces
    for j in range(pieces):
        columns = slice(j * step, (j + 1) * step)
        partial = lax.dot_general(gate_delta, gate_ref[columns, :], across, preferred_element_type=F32)
        partial += lax.dot_general(up_delta, up_ref[columns, :], across, preferred_element_type=F32)
        for p in range(peers):
            outs[j][p] = partial[p * rows : (p + 1) * rows].astype(BF16)


def experts_of(token_rows, cotan_rows, w_gate, w_upper, w_down, pieces):
    peers, owned, rows, width = token_rows.shape
    hidden = w_gate.shape[2]
    row_spec = pl.BlockSpec((peers, None, rows, width), lambda e: (0, e, 0, 0))
    step = width // pieces
    outs = [jax.ShapeDtypeStruct((peers, owned, rows, step), BF16)] * pieces
    out_specs = [pl.BlockSpec((peers, None, rows, step), lambda e: (0, e, 0, 0))] * pieces
    outs.append(jax.ShapeDtypeStruct((owned, peers * rows, 1), F32))
    out_specs.append(pl.BlockSpec((None, peers * rows, 1), lambda e: (e, 0, 0)))
    *partial, gate = call(
        functools.partial(expert_kernel, pieces),
        outs,
        (owned,),
        [
            row_spec,
            row_spec,
            pl.BlockSpec((None, width, hidden), lambda e: (e, 0, 0)),
            pl.BlockSpec((None, width, hidden), lambda e: (e, 0, 0)),
            pl.BlockSpec((None, hidden, width), lambda e: (e, 0, 0)),
        ],
        out_specs,
        10 * owned * peers * rows * width * hidden,
        6 * owned * width * hidden + 6 * owned * peers * rows * width,
    )(token_rows, cotan_rows, w_gate, w_upper, w_down)
    return partial, gate


def combine_kernel(parts, high_ref, low_ref, slots_ref, *outs):
    tokens = outs[0].shape[0]
    rows = slots_ref[...]
    total = jnp.dot(high_ref[...], rows, preferred_element_type=F32)
    total += jnp.dot(low_ref[...], rows, preferred_element_type=F32)
    for part in range(parts):
        outs[part][...] = total[part * tokens : (part + 1) * tokens].astype(outs[part].dtype)


def combine(high, low, returned, dtypes):
    sources, slots = high.shape
    width = returned.shape[1]
    parts = len(dtypes)
    tokens = sources // parts
    block = math.gcd(width, 512)
    return call(
        functools.partial(combine_kernel, parts),
        [jax.ShapeDtypeStruct((tokens, width), kind) for kind in dtypes],
        (width // block,),
        [full((sources, slots)), full((sources, slots)), pl.BlockSpec((slots, block), lambda j: (0, j))],
        [pl.BlockSpec((tokens, block), lambda j: (0, j))] * parts,
        4 * slots * sources * width,
        2 * (slots + 2 * sources) * width,
    )(high, low, returned)


def gate_kernel(capacity, experts, ids_ref, gate_ref, out_ref):
    ids = ids_ref[...]
    top = ids.shape[1]
    hits, pick = picks_of(ids, 0.0, experts)
    before = earlier_picks(pick)
    slots = gate_ref.shape[1]
    slot = lax.broadcasted_iota(jnp.int32, (1, slots), 1).astype(F32)
    gate = gate_ref[...]
    for k in range(top):
        rank = jnp.sum(jnp.where(hits[k], before, 0.0), axis=1, keepdims=True)
        dest = ids[:, k : k + 1] * capacity + rank
        out_ref[:, k : k + 1] = jnp.sum(jnp.where(slot == dest, gate, 0.0), axis=1, keepdims=True)


def gates_home(ids, gate, capacity, experts):
    tokens, top = ids.shape
    return call(
        functools.partial(gate_kernel, capacity, experts),
        jax.ShapeDtypeStruct((tokens, top), F32),
        (),
        [pl.BlockSpec(memory_space=pltpu.VMEM)] * 2,
        pl.BlockSpec(memory_space=pltpu.VMEM),
        3 * tokens * top * gate.shape[1],
        4 * tokens * top,
    )(ids, gate)


def local(tokens, cotangent, routing, expert_ids, gate_weight, up_weight, down_weight):
    count_ep = lax.axis_size("ep")
    owned = gate_weight.shape[0]
    experts = owned * count_ep
    tok_rows, top_picks = expert_ids.shape
    width = tokens.shape[1]
    capacity = 5 * tok_rows * top_picks // (4 * experts)

    peers = math.gcd(count_ep, 8)
    layers = count_ep // peers
    in_layer = [[layer * peers + i for i in range(peers)] for layer in range(layers)]
    parts = min(layers, 8 // math.gcd(8, capacity))
    chunks = [list(range(first, first + parts)) for first in range(0, layers, parts)]
    tail_pieces = 2

    def shift(value, by):
        pairs = [(i, (i + by * peers) % count_ep) for i in range(count_ep)]
        return lax.ppermute(value, "ep", pairs)

    def exchange(value):
        return lax.all_to_all(value, "ep", 0, 0, tiled=True, axis_index_groups=in_layer)

    layer = lax.axis_index("ep") // peers
    base = (layer * (peers * owned)).astype(F32).reshape(1, 1)
    ids = expert_ids.astype(F32)
    meta = jnp.concatenate([ids, routing], axis=1)
    metas = [meta] + [shift(meta, by) for by in range(1, layers)]
    token_at, cotan_at = {0: tokens}, {0: cotangent}
    for chunk in chunks:
        for by in chunk:
            if by:
                token_at[by] = shift(tokens, by)
        for by in chunk:
            if by:
                cotan_at[by] = shift(cotangent, by)

    plans, received = [], []
    for chunk in chunks:
        matrix, high, low = plan(base, jnp.stack([metas[by] for by in chunk]), owned, peers, capacity)
        plans.append((high, low))
        shape = (peers, owned * parts * capacity, width)
        token_rows = exchange(pack(matrix, [token_at[by] for by in chunk]).reshape(shape))
        cotan_rows = exchange(pack(matrix, [cotan_at[by] for by in chunk]).reshape(shape))
        received.append((token_rows, cotan_rows))

    gates, home = [], {}
    for number, chunk in enumerate(chunks):
        pieces = tail_pieces if number == len(chunks) - 1 else 1
        shape = (peers, owned, parts * capacity, width)
        token_rows, cotan_rows = [rows.reshape(shape) for rows in received[number]]
        partial, gate = experts_of(token_rows, cotan_rows, gate_weight, up_weight, down_weight, pieces)
        gates.append(gate.reshape(owned, peers, parts, capacity))
        high, low = plans[number]
        for j, piece in enumerate(partial):
            step = piece.shape[3]
            returned = exchange(piece.reshape(peers, owned * parts * capacity, step))
            kinds = [F32 if by == 0 else BF16 for by in chunk]
            sums = combine(high, low, returned.reshape(-1, step), kinds)
            for by, rows in zip(chunk, sums):
                back = rows if by == 0 else shift(rows, -by)
                home.setdefault(by, []).append(back)

    gate_slots = jnp.concatenate(gates, axis=2).transpose(2, 1, 0, 3)
    order = lax.rem(layer - jnp.arange(layers, dtype=jnp.int32) + layers, layers)
    gate_slots = gate_slots[order].reshape(count_ep, owned * capacity)
    gate_back = lax.all_to_all(gate_slots, "ep", 0, 0, tiled=True)
    gate_grad = gates_home(ids, gate_back.reshape(1, experts * capacity), capacity, experts)

    columns = []
    step = width // tail_pieces
    for j in range(tail_pieces):
        total = None
        for by in range(layers):
            rows = home[by]
            value = rows[j] if len(rows) > 1 else rows[0][:, j * step : (j + 1) * step]
            value = value.astype(F32)
            total = value if total is None else total + value
        columns.append(total)
    input_grad = jnp.concatenate(columns, axis=1)
    if lax.axis_size("hid") > 1:
        input_grad = lax.psum_scatter(input_grad, "hid", scatter_dimension=1, tiled=True)
        gate_grad = lax.psum(gate_grad, "hid")
    return (input_grad, gate_grad)


def solution(mesh):
    placed = (
        P(("rep", "ep"), None),
        P(("rep", "ep"), None),
        P(("rep", "ep"), None),
        P(("rep", "ep"), None),
        P("ep", None, "hid"),
        P("ep", None, "hid"),
        P("ep", "hid", None),
    )
    return jax.shard_map(
        local,
        mesh=mesh,
        in_specs=placed,
        out_specs=(P(("rep", "ep"), "hid"), P(("rep", "ep"), None)),
        check_vma=False,
    )
```

```python
import functools
import math

import jax
import jax.numpy as jnp
from jax import lax
from jax.experimental import pallas as pl
from jax.experimental.pallas import tpu as pltpu
from jax.sharding import PartitionSpec as P

BF16 = jnp.bfloat16
F32 = jnp.float32
LANES = 128
VMEM_LIMIT = 56 * 1024 * 1024


def full(shape):
    return pl.BlockSpec(shape, lambda *_: (0,) * len(shape))


def call(kernel, out_shape, grid, in_specs, out_specs, flops, moved, waits=()):
    count = len(in_specs)

    def body(*refs):
        kernel(*refs[:count], *refs[count + len(waits) :])

    run = pl.pallas_call(
        body,
        out_shape=out_shape,
        grid=grid,
        in_specs=[*in_specs, *[pl.BlockSpec(memory_space=pl.ANY)] * len(waits)],
        out_specs=out_specs,
        cost_estimate=pl.CostEstimate(flops=flops, bytes_accessed=moved, transcendentals=0),
        compiler_params=pltpu.CompilerParams(vmem_limit_bytes=VMEM_LIMIT),
    )
    return lambda *args: run(*args, *waits)


def picks_of(ids, base, experts):
    tokens, top = ids.shape
    expert = lax.broadcasted_iota(jnp.int32, (tokens, experts), 1).astype(F32) + base
    hits = [ids[:, k : k + 1] == expert for k in range(top)]
    return hits, functools.reduce(jnp.logical_or, hits)


def earlier_picks(pick):
    tokens = pick.shape[0]
    row = lax.broadcasted_iota(jnp.int32, (tokens, tokens), 0)
    column = lax.broadcasted_iota(jnp.int32, (tokens, tokens), 1)
    below = jnp.where(column < row, 1.0, 0.0).astype(BF16)
    return jnp.dot(below, jnp.where(pick, 1.0, 0.0).astype(BF16), preferred_element_type=F32)


def plan_kernel(shared, top, capacity, place_ref, *refs):
    meta_refs, (pack_ref, high_ref, low_ref) = refs[:-3], refs[-3:]
    parts, tokens = len(meta_refs), meta_refs[0].shape[0]
    slots = pack_ref.shape[0]
    experts = slots // (parts * capacity)
    base = (place_ref[0, 0] * experts).astype(F32)
    slot = lax.broadcasted_iota(jnp.int32, (1, slots), 1)
    rank_of = (slot % capacity).astype(F32)
    part_of = (slot // capacity) % parts
    shared_of = (slot // (capacity * parts)) % shared
    chip_of = (slot // (capacity * parts * shared)) ^ place_ref[0, 1]
    expert = lax.broadcasted_iota(jnp.int32, (experts, slots), 0)
    spread = jnp.where(expert == chip_of * shared + shared_of, 1.0, 0.0).astype(BF16)
    for part, meta_ref in enumerate(meta_refs):
        meta = meta_ref[...].astype(F32)
        hits, pick = picks_of(meta[:, :top], base, experts)
        rank = jnp.where(pick, earlier_picks(pick), -1.0).astype(BF16)
        ranks = jnp.dot(rank, spread, preferred_element_type=F32)
        here = jnp.logical_and(ranks == rank_of, part_of == part)
        rows = slice(part * tokens, (part + 1) * tokens)
        for out, first in ((high_ref, top), (low_ref, 2 * top)):
            terms = [jnp.where(hits[k], meta[:, first + k : first + k + 1], 0.0) for k in range(top)]
            term = functools.reduce(jnp.add, terms).astype(BF16)
            spread_term = jnp.dot(term, spread, preferred_element_type=F32)
            out[rows, :] = jnp.where(here, spread_term, 0.0).astype(BF16)
        pack_ref[:, rows] = jnp.where(here, 1.0, 0.0).T.astype(BF16)


def plan(place, rows, width, top, shared, chips, capacity):
    parts, tokens = len(rows), rows[0].shape[0]
    slots = chips * shared * parts * capacity
    sources = parts * tokens
    outs = (
        jax.ShapeDtypeStruct((slots, sources), BF16),
        jax.ShapeDtypeStruct((sources, slots), BF16),
        jax.ShapeDtypeStruct((sources, slots), BF16),
    )
    return call(
        functools.partial(plan_kernel, shared, top, capacity),
        outs,
        (1,),
        [pl.BlockSpec(memory_space=pltpu.SMEM)]
        + [pl.BlockSpec((tokens, LANES), lambda i: (0, width // LANES))] * parts,
        [full((slots, sources)), full((sources, slots)), full((sources, slots))],
        8 * slots * sources,
        6 * slots * sources,
    )(place, *rows)


def pack_kernel(sources, pack_ref, *refs):
    tokens = refs[0].shape[0]
    total = None
    for part, ref in enumerate(refs[:sources]):
        term = jnp.dot(
            pack_ref[:, part * tokens : (part + 1) * tokens], ref[...], preferred_element_type=F32
        )
        total = term if total is None else total + term
    first = 0
    for out_ref in refs[sources:]:
        for e in range(out_ref.shape[0]):
            rows = out_ref.shape[1]
            out_ref[e] = total[first : first + rows].astype(out_ref.dtype)
            first += rows


def pack(matrix, rows, width, chips, shared, waits):
    slots, sources = matrix.shape
    tokens = rows[0].shape[0]
    block = math.gcd(width, 512)
    depth = slots // (chips * shared)
    return call(
        functools.partial(pack_kernel, len(rows)),
        [jax.ShapeDtypeStruct((shared, depth, width), rows[0].dtype)] * chips,
        (width // block,),
        [full((slots, sources))] + [pl.BlockSpec((tokens, block), lambda j: (0, j))] * len(rows),
        [pl.BlockSpec((shared, depth, block), lambda j: (0, 0, j))] * chips,
        2 * slots * sources * width,
        2 * (slots + sources) * width,
        waits,
    )(matrix, *rows)


def expert_body(pieces, token_refs, cotan_refs, gate_ref, up_ref, down_ref, outs, gate_out):
    rows, width = token_refs[0].shape

    def joined(refs):
        return jnp.concatenate([ref[...].astype(F32) for ref in refs], axis=0).astype(BF16)

    inputs, grads_in = joined(token_refs), joined(cotan_refs)
    gate_pre = jnp.dot(inputs, gate_ref[...], preferred_element_type=F32)
    up_pre = jnp.dot(inputs, up_ref[...], preferred_element_type=F32)
    across = (((1,), (1,)), ((), ()))
    upward = lax.dot_general(grads_in, down_ref[...], across, preferred_element_type=F32)
    sigma = 1.0 / (1.0 + jnp.exp(-gate_pre))
    silu_val = gate_pre * sigma
    gate_out[...] = jnp.sum(silu_val * up_pre * upward, axis=1, keepdims=True)
    gate_delta = (upward * up_pre * sigma * (1.0 + gate_pre * (1.0 - sigma))).astype(BF16)
    up_delta = (upward * silu_val).astype(BF16)
    step = width // pieces
    chips = len(token_refs)
    for j in range(pieces):
        columns = slice(j * step, (j + 1) * step)
        partial = lax.dot_general(gate_delta, gate_ref[columns, :], across, preferred_element_type=F32)
        partial += lax.dot_general(up_delta, up_ref[columns, :], across, preferred_element_type=F32)
        for chip in range(chips):
            outs[j * chips + chip][...] = partial[chip * rows : (chip + 1) * rows].astype(BF16)


def expert_kernel(chips, pieces, owned, *refs):
    token_refs, cotan_refs = refs[:chips], refs[chips : 2 * chips]
    outs = refs[-1 - pieces * chips : -1]
    weights = refs[2 * chips : -1 - pieces * chips]
    for number in range(len(weights) // 3):

        @pl.when(pl.program_id(0) // owned == number)
        def _(number=number):
            own = weights[3 * number : 3 * number + 3]
            expert_body(pieces, token_refs, cotan_refs, *own, outs, refs[-1])


def experts_of(token_rows, cotan_rows, weights, pieces, waits):
    chips = len(token_rows)
    shared, rows, width = token_rows[0].shape
    owned, _, hidden = weights[0][0].shape
    row_spec = pl.BlockSpec((None, rows, width), lambda e: (e, 0, 0))
    step = width // pieces
    outs = [jax.ShapeDtypeStruct((shared, rows, step), BF16)] * (pieces * chips)
    out_specs = [pl.BlockSpec((None, rows, step), lambda e: (e, 0, 0))] * (pieces * chips)
    outs.append(jax.ShapeDtypeStruct((shared, chips * rows, 1), F32))
    out_specs.append(pl.BlockSpec((None, chips * rows, 1), lambda e: (e, 0, 0)))
    weight_specs = []
    for number in range(len(weights)):

        def place(e, number=number):
            return (jnp.clip(e - number * owned, 0, owned - 1), 0, 0)

        weight_specs += [pl.BlockSpec((None, width, hidden), place)] * 2
        weight_specs.append(pl.BlockSpec((None, hidden, width), place))
    *partial, gate = call(
        functools.partial(expert_kernel, chips, pieces, owned),
        outs,
        (shared,),
        [row_spec] * (2 * chips) + weight_specs,
        out_specs,
        10 * shared * chips * rows * width * hidden,
        6 * shared * width * hidden + 6 * shared * chips * rows * width,
        waits,
    )(*token_rows, *cotan_rows, *[w for own in weights for w in own])
    return [partial[j * chips : (j + 1) * chips] for j in range(pieces)], gate


def combine_kernel(parts, chips, high_ref, low_ref, *refs):
    outs = refs[chips:]
    tokens = outs[0].shape[0]
    total = None
    for chip, ref in enumerate(refs[:chips]):
        rows = ref[...]
        slots = slice(chip * rows.shape[0], (chip + 1) * rows.shape[0])
        for matrix in (high_ref, low_ref):
            term = jnp.dot(matrix[:, slots], rows, preferred_element_type=F32)
            total = term if total is None else total + term
    for part in range(parts):
        outs[part][...] = total[part * tokens : (part + 1) * tokens].astype(outs[part].dtype)


def combine(high, low, returned, dtypes, waits):
    sources, slots = high.shape
    depth, width = returned[0].shape
    parts, chips = len(dtypes), len(returned)
    tokens = sources // parts
    block = math.gcd(width, 512)
    return call(
        functools.partial(combine_kernel, parts, chips),
        [jax.ShapeDtypeStruct((tokens, width), kind) for kind in dtypes],
        (width // block,),
        [full((sources, slots))] * 2 + [pl.BlockSpec((depth, block), lambda j: (0, j))] * chips,
        [pl.BlockSpec((tokens, block), lambda j: (0, j))] * parts,
        4 * slots * sources * width,
        2 * (slots + 2 * sources) * width,
        waits,
    )(high, low, *returned)


def gate_kernel(capacity, experts, ids_ref, gate_ref, out_ref):
    ids = ids_ref[...]
    top = ids.shape[1]
    hits, pick = picks_of(ids, 0.0, experts)
    before = earlier_picks(pick)
    slots = gate_ref.shape[1]
    slot = lax.broadcasted_iota(jnp.int32, (1, slots), 1).astype(F32)
    gate = gate_ref[...]
    for k in range(top):
        rank = jnp.sum(jnp.where(hits[k], before, 0.0), axis=1, keepdims=True)
        dest = ids[:, k : k + 1] * capacity + rank
        out_ref[:, k : k + 1] = jnp.sum(jnp.where(slot == dest, gate, 0.0), axis=1, keepdims=True)


def gates_home(ids, gate, capacity, experts):
    tokens, top = ids.shape
    return call(
        functools.partial(gate_kernel, capacity, experts),
        jax.ShapeDtypeStruct((tokens, top), F32),
        (),
        [pl.BlockSpec(memory_space=pltpu.VMEM)] * 2,
        pl.BlockSpec(memory_space=pltpu.VMEM),
        3 * tokens * top * gate.shape[1],
        4 * tokens * top,
    )(ids, gate)


def local(tokens, cotangent, routing, expert_ids, gate_weight, up_weight, down_weight):
    count_ep = lax.axis_size("ep")
    owned = gate_weight.shape[0]
    experts = owned * count_ep
    tok_rows, top_picks = expert_ids.shape
    width = tokens.shape[1]
    capacity = 5 * tok_rows * top_picks // (4 * experts)

    cores = math.gcd(count_ep, 2)
    chips = math.gcd(count_ep // cores, 4)
    layers = count_ep // (cores * chips)
    shared = cores * owned
    parts = min(layers, 8 // math.gcd(8, capacity))
    chunks = [list(range(first, first + parts)) for first in range(0, layers, parts)]
    tail_pieces = 2

    def permute(value, target):
        return lax.ppermute(value, "ep", [(i, target(i)) for i in range(count_ep)])

    def shift(value, by):
        return permute(value, lambda i: (i + by * chips * cores) % count_ep)

    def across(values):
        return [values[0]] + [permute(values[m], lambda i: i ^ (m * cores)) for m in range(1, chips)]

    me = lax.axis_index("ep")
    core, chip, layer = me % cores, me // cores % chips, me // (cores * chips)
    place = jnp.stack([layer, chip]).reshape(1, 2)
    ids = ((expert_ids // owned) ^ core) * owned + expert_ids % owned
    ids = ids.astype(F32)
    high = lax.reduce_precision(routing, exponent_bits=8, mantissa_bits=7)
    low = (routing - high).astype(BF16)
    spare = jnp.zeros((tok_rows, LANES - 3 * top_picks), BF16)
    tagged = jnp.concatenate([tokens, ids.astype(BF16), high.astype(BF16), low, spare], axis=1)
    weights = [(gate_weight, up_weight, down_weight)]
    if cores > 1:
        weights.append(tuple(permute(w, lambda i: i ^ 1) for w in weights[0]))

    received, waits = [], list(weights[-1])
    plans, at = [], [[tagged], [cotangent]]
    for chunk in chunks:
        for rows in at:
            for by in chunk:
                if by:
                    rows.append(shift(rows[-1], 1))
            parts_rows = [rows[by] for by in chunk]
            if rows is at[0]:
                plans.append(plan(place, parts_rows, width, top_picks, shared, chips, capacity))
            packed = pack(plans[-1][0], parts_rows, width, chips, shared, waits)
            received.append(across(packed))
            waits = [packed[0]] if len(received) == 1 else [packed[0], *received[-2][1:]]

    gates, partials = [], []
    for number in range(len(chunks)):
        pieces = tail_pieces if number == len(chunks) - 1 else 1
        waits = [packed[0]] if number < len(chunks) - 1 else []
        partial, gate = experts_of(received[2 * number], received[2 * number + 1], weights, pieces, waits)
        gates.append(gate.reshape(shared, chips, parts, capacity))
        partials.append(partial)

    gate_slots = jnp.concatenate(gates, axis=2).transpose(2, 1, 0, 3)
    order = lax.rem(layer - jnp.arange(layers, dtype=jnp.int32) + layers, layers)
    gate_slots = gate_slots[order][:, jnp.arange(chips, dtype=jnp.int32) ^ chip]
    gate_slots = gate_slots.reshape(layers * chips, shared * capacity)
    same_core = [[i * cores + c for i in range(layers * chips)] for c in range(cores)]
    gate_back = lax.all_to_all(gate_slots, "ep", 0, 0, tiled=True, axis_index_groups=same_core)
    gate_grad = gates_home(ids, gate_back.reshape(1, experts * capacity), capacity, experts)

    home, waits = {}, []
    for chunk, (_, high, low), pieces in zip(chunks, plans, partials):
        for blocks in pieces:
            step = blocks[0].shape[2]
            returned = [rows.reshape(-1, step) for rows in across(blocks)]
            kinds = [F32 if by == 0 else BF16 for by in chunk]
            sums = combine(high, low, returned, kinds, waits)
            waits = [sums[0], gate_back] if chunk is chunks[0] else [sums[0]]
            for by, rows in zip(chunk, sums):
                back = rows if by == 0 else shift(rows, -by)
                home.setdefault(by, []).append(back)

    columns = []
    step = width // tail_pieces
    for j in range(tail_pieces):
        total = None
        for by in range(layers):
            rows = home[by]
            value = rows[j] if len(rows) > 1 else rows[0][:, j * step : (j + 1) * step]
            value = value.astype(F32)
            total = value if total is None else total + value
        columns.append(total)
    input_grad = jnp.concatenate(columns, axis=1)
    if lax.axis_size("hid") > 1:
        input_grad = lax.psum_scatter(input_grad, "hid", scatter_dimension=1, tiled=True)
        gate_grad = lax.psum(gate_grad, "hid")
    return (input_grad, gate_grad)


def solution(mesh):
    placed = (
        P(("rep", "ep"), None),
        P(("rep", "ep"), None),
        P(("rep", "ep"), None),
        P(("rep", "ep"), None),
        P("ep", None, "hid"),
        P("ep", None, "hid"),
        P("ep", "hid", None),
    )
    return jax.shard_map(
        local,
        mesh=mesh,
        in_specs=placed,
        out_specs=(P(("rep", "ep"), "hid"), P(("rep", "ep"), None)),
        check_vma=False,
    )
```

```python
import functools
import math

import jax
import jax.numpy as jnp
from jax import lax
from jax.experimental import pallas as pl
from jax.experimental.pallas import tpu as pltpu
from jax.sharding import PartitionSpec as P

BF16 = jnp.bfloat16
F32 = jnp.float32
ACROSS = (((1,), (1,)), ((), ()))
LANES = 128
SMALL_VMEM = 12 * 1024 * 1024
VMEM_LIMIT = 40 * 1024 * 1024


def full(shape):
    return pl.BlockSpec(shape, lambda *_: (0,) * len(shape))


def call(kernel, out_shape, grid, in_specs, out_specs, flops, moved, waits=(), scratch=(), vmem=SMALL_VMEM):
    count = len(in_specs)

    def body(*refs):
        kernel(*refs[:count], *refs[count + len(waits) :])

    run = pl.pallas_call(
        body,
        out_shape=out_shape,
        grid=grid,
        in_specs=[*in_specs, *[pl.BlockSpec(memory_space=pl.ANY)] * len(waits)],
        out_specs=out_specs,
        cost_estimate=pl.CostEstimate(flops=flops, bytes_accessed=moved, transcendentals=0),
        scratch_shapes=scratch,
        compiler_params=pltpu.CompilerParams(vmem_limit_bytes=vmem),
    )
    return lambda *args: run(*args, *waits)


def tie(value, waits):
    anywhere = pl.BlockSpec(memory_space=pl.ANY)
    return pl.pallas_call(
        lambda *refs: None,
        out_shape=jax.ShapeDtypeStruct(value.shape, value.dtype),
        in_specs=[anywhere] * (1 + len(waits)),
        out_specs=anywhere,
        input_output_aliases={0: 0},
    )(value, *waits)


def picks_of(ids, base, experts):
    tokens, top = ids.shape
    expert = lax.broadcasted_iota(jnp.int32, (tokens, experts), 1).astype(F32) + base
    hits = [ids[:, k : k + 1] == expert for k in range(top)]
    return hits, functools.reduce(jnp.logical_or, hits)


def earlier_picks(pick):
    tokens = pick.shape[0]
    row = lax.broadcasted_iota(jnp.int32, (tokens, tokens), 0)
    column = lax.broadcasted_iota(jnp.int32, (tokens, tokens), 1)
    below = jnp.where(column < row, 1.0, 0.0).astype(BF16)
    return jnp.dot(below, jnp.where(pick, 1.0, 0.0).astype(BF16), preferred_element_type=F32)


def plan_kernel(shared, top, capacity, place_ref, *refs):
    meta_refs, (pack_ref, high_ref, low_ref) = refs[:-3], refs[-3:]
    parts, tokens = len(meta_refs), meta_refs[0].shape[0]
    slots = pack_ref.shape[0]
    experts = slots // (parts * capacity)
    base = (place_ref[0, 0] * experts).astype(F32)
    slot = lax.broadcasted_iota(jnp.int32, (1, slots), 1)
    rank_of = (slot % capacity).astype(F32)
    part_of = (slot // capacity) % parts
    shared_of = (slot // (capacity * parts)) % shared
    chip_of = (slot // (capacity * parts * shared)) ^ place_ref[0, 1]
    expert = lax.broadcasted_iota(jnp.int32, (experts, slots), 0)
    spread = jnp.where(expert == chip_of * shared + shared_of, 1.0, 0.0).astype(BF16)
    for part, meta_ref in enumerate(meta_refs):
        meta = meta_ref[...].astype(F32)
        hits, pick = picks_of(meta[:, :top], base, experts)
        rank = jnp.where(pick, earlier_picks(pick), -1.0).astype(BF16)
        ranks = jnp.dot(rank, spread, preferred_element_type=F32)
        here = jnp.logical_and(ranks == rank_of, part_of == part)
        rows = slice(part * tokens, (part + 1) * tokens)
        for out, first in ((high_ref, top), (low_ref, 2 * top)):
            terms = [jnp.where(hits[k], meta[:, first + k : first + k + 1], 0.0) for k in range(top)]
            term = functools.reduce(jnp.add, terms).astype(BF16)
            spread_term = jnp.dot(term, spread, preferred_element_type=F32)
            out[rows, :] = jnp.where(here, spread_term, 0.0).astype(BF16)
        pack_ref[:, rows] = jnp.where(here, 1.0, 0.0).T.astype(BF16)


def plan(place, rows, width, top, shared, chips, capacity):
    parts, tokens = len(rows), rows[0].shape[0]
    slots = chips * shared * parts * capacity
    sources = parts * tokens
    outs = (
        jax.ShapeDtypeStruct((slots, sources), BF16),
        jax.ShapeDtypeStruct((sources, slots), BF16),
        jax.ShapeDtypeStruct((sources, slots), BF16),
    )
    return call(
        functools.partial(plan_kernel, shared, top, capacity),
        outs,
        (1,),
        [pl.BlockSpec(memory_space=pltpu.SMEM)]
        + [pl.BlockSpec((tokens, LANES), lambda i: (0, width // LANES))] * parts,
        [full((slots, sources)), full((sources, slots)), full((sources, slots))],
        8 * slots * sources,
        6 * slots * sources,
    )(place, *rows)


def pack_kernel(sources, pack_ref, *refs):
    tokens = refs[0].shape[0]
    total = None
    for part, ref in enumerate(refs[:sources]):
        term = jnp.dot(
            pack_ref[:, part * tokens : (part + 1) * tokens], ref[...], preferred_element_type=F32
        )
        total = term if total is None else total + term
    first = 0
    for out_ref in refs[sources:]:
        for e in range(out_ref.shape[0]):
            rows = out_ref.shape[1]
            out_ref[e] = total[first : first + rows].astype(out_ref.dtype)
            first += rows


def pack(matrix, rows, width, chips, shared, waits):
    slots, sources = matrix.shape
    tokens = rows[0].shape[0]
    block = math.gcd(width, 512)
    depth = slots // (chips * shared)
    return call(
        functools.partial(pack_kernel, len(rows)),
        [jax.ShapeDtypeStruct((shared, depth, width), rows[0].dtype)] * chips,
        (width // block,),
        [full((slots, sources))] + [pl.BlockSpec((tokens, block), lambda j: (0, j))] * len(rows),
        [pl.BlockSpec((shared, depth, block), lambda j: (0, 0, j))] * chips,
        2 * slots * sources * width,
        2 * (slots + sources) * width,
        waits,
    )(matrix, *rows)


def joined(refs):
    return jnp.concatenate([ref[...].astype(F32) for ref in refs], axis=0).astype(BF16)


def expert_kernel(chips, pieces, owned, owners, *refs):
    token_refs, cotan_refs = refs[:chips], refs[chips : 2 * chips]
    sources = refs[2 * chips : 2 * chips + 3 * owners]
    outs, gate_out = refs[2 * chips + 3 * owners : -5], refs[-5]
    buffers, sems = refs[-4:-1], refs[-1]
    step, steps = pl.program_id(0), pl.num_programs(0)
    slot = lax.rem(step, 2)

    def fetch(number, at, kind, into):
        return pltpu.make_async_copy(sources[3 * number + kind].at[at], buffers[kind].at[into], sems.at[into, kind])

    def start(expert, into):
        for number in range(owners):

            @pl.when(expert // owned == number)
            def _(number=number):
                for kind in range(3):
                    fetch(number, lax.rem(expert, owned), kind, into).start()

    @pl.when(step == 0)
    def _():
        start(step, slot)

    @pl.when(step + 1 < steps)
    def _():
        start(step + 1, 1 - slot)

    def weight(kind):
        fetch(0, 0, kind, slot).wait()
        return buffers[kind].at[slot]

    inputs, grads_in = joined(token_refs), joined(cotan_refs)
    gate_ref = weight(0)
    gate_pre = jnp.dot(inputs, gate_ref[...], preferred_element_type=F32)
    up_ref = weight(1)
    up_pre = jnp.dot(inputs, up_ref[...], preferred_element_type=F32)
    down_ref = weight(2)
    upward = lax.dot_general(grads_in, down_ref[...], ACROSS, preferred_element_type=F32)
    sigma = 1.0 / (1.0 + jnp.exp(-gate_pre))
    silu_val = gate_pre * sigma
    gate_out[...] = jnp.sum(silu_val * up_pre * upward, axis=1, keepdims=True)
    gate_delta = (upward * up_pre * sigma * (1.0 + gate_pre * (1.0 - sigma))).astype(BF16)
    up_delta = (upward * silu_val).astype(BF16)
    width, rows = inputs.shape[1] // pieces, inputs.shape[0] // chips
    for j in range(pieces):
        columns = slice(j * width, (j + 1) * width)
        partial = lax.dot_general(gate_delta, gate_ref[columns, :], ACROSS, preferred_element_type=F32)
        partial += lax.dot_general(up_delta, up_ref[columns, :], ACROSS, preferred_element_type=F32)
        for chip in range(chips):
            outs[j * chips + chip][...] = partial[chip * rows : (chip + 1) * rows].astype(BF16)


def experts_of(token_rows, cotan_rows, weights, pieces, waits):
    chips = len(token_rows)
    shared, rows, width = token_rows[0].shape
    owned, _, hidden = weights[0][0].shape
    all_rows, step = chips * rows, width // pieces
    row_spec = pl.BlockSpec((None, rows, width), lambda e: (e, 0, 0))
    outs = [jax.ShapeDtypeStruct((shared, rows, step), BF16)] * (pieces * chips)
    out_specs = [pl.BlockSpec((None, rows, step), lambda e: (e, 0, 0))] * (pieces * chips)
    outs.append(jax.ShapeDtypeStruct((shared, all_rows, 1), F32))
    out_specs.append(pl.BlockSpec((None, all_rows, 1), lambda e: (e, 0, 0)))
    *partial, gate = call(
        functools.partial(expert_kernel, chips, pieces, owned, len(weights)),
        outs,
        (shared,),
        [row_spec] * (2 * chips) + [pl.BlockSpec(memory_space=pl.ANY)] * (3 * len(weights)),
        out_specs,
        10 * shared * all_rows * width * hidden,
        6 * shared * width * hidden + 6 * shared * all_rows * width,
        waits,
        [pltpu.VMEM((2, *w.shape[1:]), BF16) for w in weights[0]] + [pltpu.SemaphoreType.DMA((2, 3))],
        VMEM_LIMIT,
    )(*token_rows, *cotan_rows, *[w for own in weights for w in own])
    return [partial[j * chips : (j + 1) * chips] for j in range(pieces)], gate


def combine_kernel(parts, chips, high_ref, low_ref, *refs):
    outs = refs[chips:]
    tokens = outs[0].shape[0]
    total = None
    for chip, ref in enumerate(refs[:chips]):
        rows = ref[...]
        slots = slice(chip * rows.shape[0], (chip + 1) * rows.shape[0])
        for matrix in (high_ref, low_ref):
            term = jnp.dot(matrix[:, slots], rows, preferred_element_type=F32)
            total = term if total is None else total + term
    for part in range(parts):
        outs[part][...] = total[part * tokens : (part + 1) * tokens].astype(outs[part].dtype)


def combine(high, low, returned, dtypes, waits):
    sources, slots = high.shape
    depth, width = returned[0].shape
    parts, chips = len(dtypes), len(returned)
    tokens = sources // parts
    block = math.gcd(width, 512)
    return call(
        functools.partial(combine_kernel, parts, chips),
        [jax.ShapeDtypeStruct((tokens, width), kind) for kind in dtypes],
        (width // block,),
        [full((sources, slots))] * 2 + [pl.BlockSpec((depth, block), lambda j: (0, j))] * chips,
        [pl.BlockSpec((tokens, block), lambda j: (0, j))] * parts,
        4 * slots * sources * width,
        2 * (slots + 2 * sources) * width,
        waits,
    )(high, low, *returned)


def gate_kernel(capacity, experts, ids_ref, gate_ref, out_ref):
    ids = ids_ref[...]
    top = ids.shape[1]
    hits, pick = picks_of(ids, 0.0, experts)
    before = earlier_picks(pick)
    slots = gate_ref.shape[1]
    slot = lax.broadcasted_iota(jnp.int32, (1, slots), 1).astype(F32)
    gate = gate_ref[...]
    for k in range(top):
        rank = jnp.sum(jnp.where(hits[k], before, 0.0), axis=1, keepdims=True)
        dest = ids[:, k : k + 1] * capacity + rank
        out_ref[:, k : k + 1] = jnp.sum(jnp.where(slot == dest, gate, 0.0), axis=1, keepdims=True)


def gates_home(ids, gate, capacity, experts):
    tokens, top = ids.shape
    return call(
        functools.partial(gate_kernel, capacity, experts),
        jax.ShapeDtypeStruct((tokens, top), F32),
        (),
        [pl.BlockSpec(memory_space=pltpu.VMEM)] * 2,
        pl.BlockSpec(memory_space=pltpu.VMEM),
        3 * tokens * top * gate.shape[1],
        4 * tokens * top,
    )(ids, gate)


def local(tokens, cotangent, routing, expert_ids, gate_weight, up_weight, down_weight):
    count_ep = lax.axis_size("ep")
    owned = gate_weight.shape[0]
    experts = owned * count_ep
    tok_rows, top_picks = expert_ids.shape
    width = tokens.shape[1]
    capacity = 5 * tok_rows * top_picks // (4 * experts)

    cores = math.gcd(count_ep, 2)
    chips = math.gcd(count_ep // cores, 4)
    layers = count_ep // (cores * chips)
    shared = cores * owned
    parts = min(layers, 8 // math.gcd(8, capacity))
    chunks = [list(range(first, first + parts)) for first in range(0, layers, parts)]
    tail_pieces = 2

    def permute(value, target):
        return lax.ppermute(value, "ep", [(i, target(i)) for i in range(count_ep)])

    def shift(value, by):
        return permute(value, lambda i: (i + by * chips * cores) % count_ep)

    def across(values):
        return [values[0]] + [permute(values[m], lambda i: i ^ (m * cores)) for m in range(1, chips)]

    me = lax.axis_index("ep")
    core, chip, layer = me % cores, me // cores % chips, me // (cores * chips)
    place = jnp.stack([layer, chip]).reshape(1, 2)
    ids = ((expert_ids // owned) ^ core) * owned + expert_ids % owned
    ids = ids.astype(F32)
    high = lax.reduce_precision(routing, exponent_bits=8, mantissa_bits=7)
    low = (routing - high).astype(BF16)
    spare = jnp.zeros((tok_rows, LANES - 3 * top_picks), BF16)
    tagged = jnp.concatenate([tokens, ids.astype(BF16), high.astype(BF16), low, spare], axis=1)
    weights = [(gate_weight, up_weight, down_weight)]
    if cores > 1:
        weights.append(tuple(permute(w, lambda i: i ^ 1) for w in weights[0]))

    received, waits = [], list(weights[-1])
    plans, at = [], [[tagged], [cotangent]]
    for chunk in chunks:
        for rows in at:
            for by in chunk:
                if by:
                    rows.append(shift(rows[-1], 1))
            parts_rows = [rows[by] for by in chunk]
            if rows is at[0]:
                plans.append(plan(place, parts_rows, width, top_picks, shared, chips, capacity))
            packed = pack(plans[-1][0], parts_rows, width, chips, shared, waits)
            received.append(across(packed))
            waits = [packed[0]] if len(received) == 1 else [packed[0], *received[-2][1:]]

    gates, partials = [], []
    for number in range(len(chunks)):
        pieces = tail_pieces if number == len(chunks) - 1 else 1
        waits = [packed[0]] if number < len(chunks) - 1 else []
        partial, gate = experts_of(received[2 * number], received[2 * number + 1], weights, pieces, waits)
        gates.append(gate.reshape(shared, chips, parts, capacity))
        partials.append(partial)

    gate_slots = jnp.concatenate(gates, axis=2).transpose(2, 1, 0, 3)
    order = lax.rem(layer - jnp.arange(layers, dtype=jnp.int32) + layers, layers)
    gate_slots = gate_slots[order][:, jnp.arange(chips, dtype=jnp.int32) ^ chip]
    gate_slots = gate_slots.reshape(layers * chips, shared * capacity)
    same_core = [[i * cores + c for i in range(layers * chips)] for c in range(cores)]
    gate_back = lax.all_to_all(gate_slots, "ep", 0, 0, tiled=True, axis_index_groups=same_core)
    gate_grad = gates_home(ids, gate_back.reshape(1, experts * capacity), capacity, experts)

    home, waits = {}, []
    for chunk, (_, high, low), pieces in zip(chunks, plans, partials):
        for blocks in pieces:
            step = blocks[0].shape[2]
            if chunk is not chunks[0] and blocks is pieces[1]:
                blocks = [blocks[0]] + [tie(rows, first_sums[:1]) for rows in blocks[1:]]
            returned = [rows.reshape(-1, step) for rows in across(blocks)]
            kinds = [F32 if by == 0 else BF16 for by in chunk]
            sums = combine(high, low, returned, kinds, waits)
            waits = [sums[0]]
            if chunk is chunks[0]:
                first_sums = sums
            elif blocks is pieces[0]:
                waits.append(gate_back)
            for by, rows in zip(chunk, sums):
                back = rows if by == 0 else shift(rows, -by)
                home.setdefault(by, []).append(back)
                if chunk is chunks[0] and by:
                    waits.append(back)

    columns = []
    step = width // tail_pieces
    for j in range(tail_pieces):
        total = None
        for by in range(layers):
            rows = home[by]
            value = rows[j] if len(rows) > 1 else rows[0][:, j * step : (j + 1) * step]
            value = value.astype(F32)
            total = value if total is None else total + value
        columns.append(total)
    input_grad = jnp.concatenate(columns, axis=1)
    if lax.axis_size("hid") > 1:
        input_grad = lax.psum_scatter(input_grad, "hid", scatter_dimension=1, tiled=True)
        gate_grad = lax.psum(gate_grad, "hid")
    return (input_grad, gate_grad)


def solution(mesh):
    placed = (
        P(("rep", "ep"), None),
        P(("rep", "ep"), None),
        P(("rep", "ep"), None),
        P(("rep", "ep"), None),
        P("ep", None, "hid"),
        P("ep", None, "hid"),
        P("ep", "hid", None),
    )
    return jax.shard_map(
        local,
        mesh=mesh,
        in_specs=placed,
        out_specs=(P(("rep", "ep"), "hid"), P(("rep", "ep"), None)),
        check_vma=False,
    )
```

```python
import functools
import math

import jax
import jax.numpy as jnp
from jax import lax
from jax.experimental import pallas as pl
from jax.experimental.pallas import tpu as pltpu
from jax.sharding import PartitionSpec as P

BF16 = jnp.bfloat16
F32 = jnp.float32
ACROSS = (((1,), (1,)), ((), ()))
LANES = 128
SMALL_VMEM = 12 * 1024 * 1024
VMEM_LIMIT = 40 * 1024 * 1024


def full(shape):
    return pl.BlockSpec(shape, lambda *_: (0,) * len(shape))


def call(kernel, out_shape, grid, in_specs, out_specs, flops, moved, waits=(), scratch=(), vmem=SMALL_VMEM):
    count = len(in_specs)

    def body(*refs):
        kernel(*refs[:count], *refs[count + len(waits) :])

    run = pl.pallas_call(
        body,
        out_shape=out_shape,
        grid=grid,
        in_specs=[*in_specs, *[pl.BlockSpec(memory_space=pl.ANY)] * len(waits)],
        out_specs=out_specs,
        cost_estimate=pl.CostEstimate(flops=flops, bytes_accessed=moved, transcendentals=0),
        scratch_shapes=scratch,
        compiler_params=pltpu.CompilerParams(vmem_limit_bytes=vmem),
    )
    return lambda *args: run(*args, *waits)


def tie(value, waits):
    anywhere = pl.BlockSpec(memory_space=pl.ANY)
    return pl.pallas_call(
        lambda *refs: None,
        out_shape=jax.ShapeDtypeStruct(value.shape, value.dtype),
        in_specs=[anywhere] * (1 + len(waits)),
        out_specs=anywhere,
        input_output_aliases={0: 0},
    )(value, *waits)


def picks_of(ids, base, experts):
    tokens, top = ids.shape
    expert = lax.broadcasted_iota(jnp.int32, (tokens, experts), 1).astype(F32) + base
    hits = [ids[:, k : k + 1] == expert for k in range(top)]
    return hits, functools.reduce(jnp.logical_or, hits)


def earlier_picks(pick):
    tokens = pick.shape[0]
    row = lax.broadcasted_iota(jnp.int32, (tokens, tokens), 0)
    column = lax.broadcasted_iota(jnp.int32, (tokens, tokens), 1)
    below = jnp.where(column < row, 1.0, 0.0).astype(BF16)
    return jnp.dot(below, jnp.where(pick, 1.0, 0.0).astype(BF16), preferred_element_type=F32)


def plan_kernel(shared, top, capacity, place_ref, *refs):
    meta_refs, (pack_ref, high_ref, low_ref) = refs[:-3], refs[-3:]
    parts, tokens = len(meta_refs), meta_refs[0].shape[0]
    slots = pack_ref.shape[0]
    experts = slots // (parts * capacity)
    base = (place_ref[0, 0] * experts).astype(F32)
    slot = lax.broadcasted_iota(jnp.int32, (1, slots), 1)
    rank_of = (slot % capacity).astype(F32)
    part_of = (slot // capacity) % parts
    shared_of = (slot // (capacity * parts)) % shared
    chip_of = (slot // (capacity * parts * shared)) ^ place_ref[0, 1]
    expert = lax.broadcasted_iota(jnp.int32, (experts, slots), 0)
    spread = jnp.where(expert == chip_of * shared + shared_of, 1.0, 0.0).astype(BF16)
    for part, meta_ref in enumerate(meta_refs):
        meta = meta_ref[...].astype(F32)
        hits, pick = picks_of(meta[:, :top], base, experts)
        rank = jnp.where(pick, earlier_picks(pick), -1.0).astype(BF16)
        ranks = jnp.dot(rank, spread, preferred_element_type=F32)
        here = jnp.logical_and(ranks == rank_of, part_of == part)
        rows = slice(part * tokens, (part + 1) * tokens)
        for out, first in ((high_ref, top), (low_ref, 2 * top)):
            terms = [jnp.where(hits[k], meta[:, first + k : first + k + 1], 0.0) for k in range(top)]
            term = functools.reduce(jnp.add, terms).astype(BF16)
            spread_term = jnp.dot(term, spread, preferred_element_type=F32)
            out[rows, :] = jnp.where(here, spread_term, 0.0).astype(BF16)
        pack_ref[:, rows] = jnp.where(here, 1.0, 0.0).T.astype(BF16)


def plan(place, rows, width, top, shared, chips, capacity):
    parts, tokens = len(rows), rows[0].shape[0]
    slots = chips * shared * parts * capacity
    sources = parts * tokens
    outs = (
        jax.ShapeDtypeStruct((slots, sources), BF16),
        jax.ShapeDtypeStruct((sources, slots), BF16),
        jax.ShapeDtypeStruct((sources, slots), BF16),
    )
    return call(
        functools.partial(plan_kernel, shared, top, capacity),
        outs,
        (1,),
        [pl.BlockSpec(memory_space=pltpu.SMEM)]
        + [pl.BlockSpec((tokens, LANES), lambda i: (0, width // LANES))] * parts,
        [full((slots, sources)), full((sources, slots)), full((sources, slots))],
        8 * slots * sources,
        6 * slots * sources,
    )(place, *rows)


def pack_kernel(sources, pack_ref, *refs):
    tokens = refs[0].shape[0]
    total = None
    for part, ref in enumerate(refs[:sources]):
        term = jnp.dot(
            pack_ref[:, part * tokens : (part + 1) * tokens], ref[...], preferred_element_type=F32
        )
        total = term if total is None else total + term
    first = 0
    for out_ref in refs[sources:]:
        for e in range(out_ref.shape[0]):
            rows = out_ref.shape[1]
            out_ref[e] = total[first : first + rows].astype(out_ref.dtype)
            first += rows


def pack(matrix, rows, width, chips, shared, waits):
    slots, sources = matrix.shape
    tokens = rows[0].shape[0]
    block = math.gcd(width, 512)
    depth = slots // (chips * shared)
    return call(
        functools.partial(pack_kernel, len(rows)),
        [jax.ShapeDtypeStruct((shared, depth, width), rows[0].dtype)] * chips,
        (width // block,),
        [full((slots, sources))] + [pl.BlockSpec((tokens, block), lambda j: (0, j))] * len(rows),
        [pl.BlockSpec((shared, depth, block), lambda j: (0, 0, j))] * chips,
        2 * slots * sources * width,
        2 * (slots + sources) * width,
        waits,
    )(matrix, *rows)


def joined(refs):
    return jnp.concatenate([ref[...].astype(F32) for ref in refs], axis=0).astype(BF16)


def expert_kernel(chips, pieces, owned, owners, *refs):
    token_refs, cotan_refs = refs[:chips], refs[chips : 2 * chips]
    sources = refs[2 * chips : 2 * chips + 3 * owners]
    outs, gate_out = refs[2 * chips + 3 * owners : -5], refs[-5]
    buffers, sems = refs[-4:-1], refs[-1]
    step, steps = pl.program_id(0), pl.num_programs(0)
    slot = lax.rem(step, 2)

    def fetch(number, at, kind, into):
        return pltpu.make_async_copy(sources[3 * number + kind].at[at], buffers[kind].at[into], sems.at[into, kind])

    def start(expert, into):
        for number in range(owners):

            @pl.when(expert // owned == number)
            def _(number=number):
                for kind in range(3):
                    fetch(number, lax.rem(expert, owned), kind, into).start()

    @pl.when(step == 0)
    def _():
        start(step, slot)

    @pl.when(step + 1 < steps)
    def _():
        start(step + 1, 1 - slot)

    def weight(kind):
        fetch(0, 0, kind, slot).wait()
        return buffers[kind].at[slot]

    inputs, grads_in = joined(token_refs), joined(cotan_refs)
    gate_ref = weight(0)
    gate_pre = jnp.dot(inputs, gate_ref[...], preferred_element_type=F32)
    up_ref = weight(1)
    up_pre = jnp.dot(inputs, up_ref[...], preferred_element_type=F32)
    down_ref = weight(2)
    upward = lax.dot_general(grads_in, down_ref[...], ACROSS, preferred_element_type=F32)
    sigma = 1.0 / (1.0 + jnp.exp(-gate_pre))
    silu_val = gate_pre * sigma
    gate_out[...] = jnp.sum(silu_val * up_pre * upward, axis=1, keepdims=True)
    gate_delta = (upward * up_pre * sigma * (1.0 + gate_pre * (1.0 - sigma))).astype(BF16)
    up_delta = (upward * silu_val).astype(BF16)
    width, rows = inputs.shape[1] // pieces, inputs.shape[0] // chips
    for j in range(pieces):
        columns = slice(j * width, (j + 1) * width)
        partial = lax.dot_general(gate_delta, gate_ref[columns, :], ACROSS, preferred_element_type=F32)
        partial += lax.dot_general(up_delta, up_ref[columns, :], ACROSS, preferred_element_type=F32)
        for chip in range(chips):
            outs[j * chips + chip][...] = partial[chip * rows : (chip + 1) * rows].astype(BF16)


def experts_of(token_rows, cotan_rows, weights, pieces, waits):
    chips = len(token_rows)
    shared, rows, width = token_rows[0].shape
    owned, _, hidden = weights[0][0].shape
    all_rows, step = chips * rows, width // pieces
    row_spec = pl.BlockSpec((None, rows, width), lambda e: (e, 0, 0))
    outs = [jax.ShapeDtypeStruct((shared, rows, step), BF16)] * (pieces * chips)
    out_specs = [pl.BlockSpec((None, rows, step), lambda e: (e, 0, 0))] * (pieces * chips)
    outs.append(jax.ShapeDtypeStruct((shared, all_rows, 1), F32))
    out_specs.append(pl.BlockSpec((None, all_rows, 1), lambda e: (e, 0, 0)))
    *partial, gate = call(
        functools.partial(expert_kernel, chips, pieces, owned, len(weights)),
        outs,
        (shared,),
        [row_spec] * (2 * chips) + [pl.BlockSpec(memory_space=pl.ANY)] * (3 * len(weights)),
        out_specs,
        10 * shared * all_rows * width * hidden,
        6 * shared * width * hidden + 6 * shared * all_rows * width,
        waits,
        [pltpu.VMEM((2, *w.shape[1:]), BF16) for w in weights[0]] + [pltpu.SemaphoreType.DMA((2, 3))],
        VMEM_LIMIT,
    )(*token_rows, *cotan_rows, *[w for own in weights for w in own])
    return [partial[j * chips : (j + 1) * chips] for j in range(pieces)], gate


def combine_kernel(parts, chips, high_ref, low_ref, *refs):
    outs = refs[chips:]
    tokens = outs[0].shape[0]
    total = None
    for chip, ref in enumerate(refs[:chips]):
        rows = ref[...]
        slots = slice(chip * rows.shape[0], (chip + 1) * rows.shape[0])
        for matrix in (high_ref, low_ref):
            term = jnp.dot(matrix[:, slots], rows, preferred_element_type=F32)
            total = term if total is None else total + term
    for part in range(parts):
        outs[part][...] = total[part * tokens : (part + 1) * tokens].astype(outs[part].dtype)


def combine(high, low, returned, dtypes, waits):
    sources, slots = high.shape
    depth, width = returned[0].shape
    parts, chips = len(dtypes), len(returned)
    tokens = sources // parts
    block = math.gcd(width, 512)
    return call(
        functools.partial(combine_kernel, parts, chips),
        [jax.ShapeDtypeStruct((tokens, width), kind) for kind in dtypes],
        (width // block,),
        [full((sources, slots))] * 2 + [pl.BlockSpec((depth, block), lambda j: (0, j))] * chips,
        [pl.BlockSpec((tokens, block), lambda j: (0, j))] * parts,
        4 * slots * sources * width,
        2 * (slots + 2 * sources) * width,
        waits,
    )(high, low, *returned)


def gate_kernel(capacity, experts, ids_ref, gate_ref, out_ref):
    ids = ids_ref[...]
    top = ids.shape[1]
    hits, pick = picks_of(ids, 0.0, experts)
    before = earlier_picks(pick)
    slots = gate_ref.shape[1]
    slot = lax.broadcasted_iota(jnp.int32, (1, slots), 1).astype(F32)
    gate = gate_ref[...]
    for k in range(top):
        rank = jnp.sum(jnp.where(hits[k], before, 0.0), axis=1, keepdims=True)
        dest = ids[:, k : k + 1] * capacity + rank
        out_ref[:, k : k + 1] = jnp.sum(jnp.where(slot == dest, gate, 0.0), axis=1, keepdims=True)


def gates_home(ids, gate, capacity, experts):
    tokens, top = ids.shape
    return call(
        functools.partial(gate_kernel, capacity, experts),
        jax.ShapeDtypeStruct((tokens, top), F32),
        (),
        [pl.BlockSpec(memory_space=pltpu.VMEM)] * 2,
        pl.BlockSpec(memory_space=pltpu.VMEM),
        3 * tokens * top * gate.shape[1],
        4 * tokens * top,
    )(ids, gate)


def home_kernel(counts, pieces, *refs):
    out = refs[-1]
    step = out.shape[1] // pieces
    for j in range(pieces):
        columns = slice(j * step, (j + 1) * step)
        total, first = None, 0
        for count in counts:
            value = refs[first + j][...] if count > 1 else refs[first][:, columns]
            value = value.astype(F32)
            total = value if total is None else total + value
            first += count
        out[:, columns] = total


def sums_home(layers_rows, width, pieces):
    flat = [rows for layer_rows in layers_rows for rows in layer_rows]
    tokens = flat[0].shape[0]
    return call(
        functools.partial(home_kernel, [len(layer_rows) for layer_rows in layers_rows], pieces),
        jax.ShapeDtypeStruct((tokens, width), F32),
        (),
        [pl.BlockSpec(memory_space=pltpu.VMEM)] * len(flat),
        pl.BlockSpec(memory_space=pltpu.VMEM),
        len(layers_rows) * tokens * width,
        4 * tokens * width,
    )(*flat)


def local(tokens, cotangent, routing, expert_ids, gate_weight, up_weight, down_weight):
    count_ep = lax.axis_size("ep")
    owned = gate_weight.shape[0]
    experts = owned * count_ep
    tok_rows, top_picks = expert_ids.shape
    width = tokens.shape[1]
    capacity = 5 * tok_rows * top_picks // (4 * experts)

    cores = math.gcd(count_ep, 2)
    chips = math.gcd(count_ep // cores, 4)
    layers = count_ep // (cores * chips)
    shared = cores * owned
    parts = min(layers, 8 // math.gcd(8, capacity))
    chunks = [list(range(first, first + parts)) for first in range(0, layers, parts)]
    tail_pieces = 2

    def permute(value, target):
        return lax.ppermute(value, "ep", [(i, target(i)) for i in range(count_ep)])

    def shift(value, by):
        return permute(value, lambda i: (i + by * chips * cores) % count_ep)

    def across(values):
        return [values[0]] + [permute(values[m], lambda i: i ^ (m * cores)) for m in range(1, chips)]

    me = lax.axis_index("ep")
    core, chip, layer = me % cores, me // cores % chips, me // (cores * chips)
    place = jnp.stack([layer, chip]).reshape(1, 2)
    ids = ((expert_ids // owned) ^ core) * owned + expert_ids % owned
    ids = ids.astype(F32)
    high = lax.reduce_precision(routing, exponent_bits=8, mantissa_bits=7)
    low = (routing - high).astype(BF16)
    spare = jnp.zeros((tok_rows, LANES - 3 * top_picks), BF16)
    tagged = jnp.concatenate([tokens, ids.astype(BF16), high.astype(BF16), low, spare], axis=1)
    weights = [(gate_weight, up_weight, down_weight)]
    if cores > 1:
        weights.append(tuple(permute(w, lambda i: i ^ 1) for w in weights[0]))

    received, waits = [], list(weights[-1])
    plans, at = [], [[tagged], [cotangent]]
    for chunk in chunks:
        for rows in at:
            for by in chunk:
                if by:
                    rows.append(shift(rows[-1], 1))
            parts_rows = [rows[by] for by in chunk]
            if rows is at[0]:
                plans.append(plan(place, parts_rows, width, top_picks, shared, chips, capacity))
            packed = pack(plans[-1][0], parts_rows, width, chips, shared, waits)
            received.append(across(packed))
            waits = [packed[0]] if len(received) == 1 else [packed[0], *received[-2][1:]]

    gates, partials = [], []
    for number in range(len(chunks)):
        pieces = tail_pieces if number == len(chunks) - 1 else 1
        waits = [packed[0]] if number < len(chunks) - 1 else []
        partial, gate = experts_of(received[2 * number], received[2 * number + 1], weights, pieces, waits)
        gates.append(gate.reshape(shared, chips, parts, capacity))
        partials.append(partial)

    gate_slots = jnp.concatenate(gates, axis=2).transpose(2, 1, 0, 3)
    order = lax.rem(layer - jnp.arange(layers, dtype=jnp.int32) + layers, layers)
    gate_slots = gate_slots[order][:, jnp.arange(chips, dtype=jnp.int32) ^ chip]
    gate_slots = gate_slots.reshape(layers * chips, shared * capacity)
    same_core = [[i * cores + c for i in range(layers * chips)] for c in range(cores)]
    gate_back = lax.all_to_all(gate_slots, "ep", 0, 0, tiled=True, axis_index_groups=same_core)
    gate_grad = gates_home(ids, gate_back.reshape(1, experts * capacity), capacity, experts)

    home, waits = {}, []
    for chunk, (_, high, low), pieces in zip(chunks, plans, partials):
        for blocks in pieces:
            step = blocks[0].shape[2]
            if chunk is not chunks[0] and blocks is pieces[1]:
                blocks = [blocks[0]] + [tie(rows, first_sums[:1]) for rows in blocks[1:]]
            returned = [rows.reshape(-1, step) for rows in across(blocks)]
            kinds = [F32 if by == 0 else BF16 for by in chunk]
            sums = combine(high, low, returned, kinds, waits)
            waits = [sums[0]]
            if chunk is chunks[0]:
                first_sums = sums
            elif blocks is pieces[0]:
                waits.append(gate_back)
            for by, rows in zip(chunk, sums):
                back = rows if by == 0 else shift(rows, -by)
                home.setdefault(by, []).append(back)
                if chunk is chunks[0] and by:
                    waits.append(back)

    input_grad = sums_home([home[by] for by in range(layers)], width, tail_pieces)
    if lax.axis_size("hid") > 1:
        input_grad = lax.psum_scatter(input_grad, "hid", scatter_dimension=1, tiled=True)
        gate_grad = lax.psum(gate_grad, "hid")
    return (input_grad, gate_grad)


def solution(mesh):
    placed = (
        P(("rep", "ep"), None),
        P(("rep", "ep"), None),
        P(("rep", "ep"), None),
        P(("rep", "ep"), None),
        P("ep", None, "hid"),
        P("ep", None, "hid"),
        P("ep", "hid", None),
    )
    return jax.shard_map(
        local,
        mesh=mesh,
        in_specs=placed,
        out_specs=(P(("rep", "ep"), "hid"), P(("rep", "ep"), None)),
        check_vma=False,
    )
```
